32 devices in a mesh: groups: 2 (over x), blk: 16 (over z, y, core).
Axes of the slice: x: 2, y: 2, z: 4, core: 2. Of those that a mesh axis runs over, the one named last changes fastest.
Arguments:
- points: float32 [16384, 32], P(('groups', 'blk')), parts along dimension 0, may hold values from -6 to 6
- targets: float32 [16384, 16], P(('groups', 'blk')), parts along dimension 0, may hold values from -8 to 8
- noise_var: float32 [16384], P(('groups', 'blk')), parts along dimension 0, may hold values from 0.3 to 3
- inv_length: float32 [32], replicated, may hold values from 0.1 to 0.5
Outputs:
- solution: float32 [16384, 16], P(('groups', 'blk')), parts along dimension 0
- residual: float32 [16384, 16], P(('groups', 'blk')), parts along dimension 0
- direction: float32 [16384, 16], P(('groups', 'blk')), parts along dimension 0
The draws below stay inside these ranges and needn't reach their ends.
There are 2 independent parts, one for each index of `groups`. The reference program is written for one: setup_inputs(seed, part) draws one part's arguments, and reference() takes and returns one part's arrays. A program takes and returns all parts, laid end to end along the dimension named above; an argument that names none is the same for every part. Nothing has to cross between parts.
All inputs are finite; a program needn't handle non-finite values.
Results may differ from the reference program's by a relative error of at most 0.0003.
Values sent between devices are 32-bit elements; how exact they have to be, the bound alone decides.
A program may use at most 64 MiB of HBM per device.

```python
import math
import jax
import jax.numpy as jnp
from jax import lax

F = 32
R = 16
ITERS = 1
P_DEV = 512
POINTS = 8192
N_BLK = 16


def draw_targets(key, part):
    key = jax.random.fold_in(key, 11)
    rising = 0.6 + 1.2 * jnp.arange(POINTS, dtype=jnp.float32) / (POINTS - 1)
    values = jnp.clip(jax.random.normal(key, (POINTS, R), jnp.float32), -4.0, 4.0)
    return values * rising[:, None]


def shard_levels(key, extent, shards, low, top_value):
    factor_of, own = 1.0, jax.random.fold_in(key, 6)
    for dim, blocks in shards:
        draws = jnp.exp(jax.random.uniform(jax.random.fold_in(own, dim), (blocks,), jnp.float32, low / len(shards), top_value / len(shards)))
        factor_of = factor_of * jnp.repeat(draws, extent[dim] // blocks).reshape([-1 if axis == dim else 1 for axis in range(len(extent))])
    return factor_of


def centred(stream_key, shape, deviation, reach, cuts=(), kind=jnp.bfloat16):
    level = shard_levels(stream_key, shape, cuts, -0.22, 0.18) if cuts else 1.0
    drawn = jax.random.normal(stream_key, shape, jnp.float32) * deviation * level
    return jnp.minimum(jnp.maximum(drawn, -reach), reach).astype(kind)


def setup_inputs(seed: int = 0, part: int = 0) -> dict:
    streams_of = jax.random.split(jax.random.key(seed), 5)
    own_keys = jax.random.split(jax.random.fold_in(streams_of[4], part), 5)
    return {
        "points": centred(own_keys[0], (POINTS, F), 1.0, 6.0, ((0, 16),), jnp.float32),
        "targets": draw_targets(jax.random.fold_in(jax.random.fold_in(streams_of[4], part), 71), part),
        "noise_var": jnp.clip(jnp.exp(math.log(3.0) - 2.3025851 * jax.random.uniform(own_keys[2], (POINTS,), jnp.float32) ** shard_levels(own_keys[2], (POINTS,), ((0, 16),), -0.2, 0.2)), 0.3, 3.0),
        "inv_length": jnp.clip(jnp.exp(jax.random.uniform(streams_of[3], (F,), jnp.float32, math.log(0.1), math.log(0.5))), 0.1, 0.5),
    }


def reference(points, targets, noise_var, inv_length):
    scaled = points * inv_length[None, :]
    sqnorm = jnp.sum(scaled * scaled, axis=1)

    def apply_kernel(vectors):
        def block_rows(index):
            offset = (index * P_DEV).astype(jnp.int32)
            near = lax.dynamic_slice_in_dim(scaled, offset, P_DEV, 0)
            near_norms = lax.dynamic_slice_in_dim(sqnorm, offset, P_DEV, 0)
            cross = lax.dot_general(near, scaled, (((1,), (1,)), ((), ())), precision=lax.Precision.HIGHEST, preferred_element_type=jnp.float32)
            kernel = jnp.exp(-0.5 * (near_norms[:, None] + sqnorm[None, :] - 2.0 * cross))
            return jnp.dot(kernel, vectors, precision=lax.Precision.HIGHEST, preferred_element_type=jnp.float32)

        blocks = lax.map(block_rows, jnp.arange(N_BLK, dtype=jnp.int32))
        return blocks.reshape(POINTS, R) + noise_var[:, None] * vectors

    solution = jnp.zeros_like(targets)
    residual = targets
    direction = targets
    norm_now = jnp.sum(residual * residual, axis=0)
    for step_index in range(ITERS):
        image = apply_kernel(direction)
        step_size = norm_now / jnp.sum(direction * image, axis=0)
        solution = solution + step_size[None, :] * direction
        residual = residual - step_size[None, :] * image
        norm_next = jnp.sum(residual * residual, axis=0)
        direction = residual + (norm_next / norm_now)[None, :] * direction
        norm_now = norm_next
    return solution, residual, direction
```

```python
import functools

import jax
import jax.numpy as jnp
from jax import lax
from jax.experimental import pallas as pl
from jax.experimental.pallas import tpu as pltpu
from jax.sharding import PartitionSpec as P

F32 = jnp.float32
BF16 = jnp.bfloat16
LOG2E = 1.4426950408889634


def split3(value):
    high = value.astype(BF16)
    rest = value - high.astype(F32)
    middle = rest.astype(BF16)
    low = (rest - middle.astype(F32)).astype(BF16)
    return high, middle, low


def augmented(scaled, near):
    count = scaled.shape[1]
    norm = -0.5 * jnp.sum(scaled * scaled, axis=0, keepdims=True)
    row = lax.broadcasted_iota(jnp.int32, (16, count), 0)
    first = 0 if near else 3
    tail = jnp.where(row < 6, 1.0, 0.0)
    for offset, part in enumerate(split3(norm)):
        spread = jnp.broadcast_to(part.astype(F32), (16, count))
        tail = jnp.where(row == first + offset, spread, tail)
    high, middle, low = split3(scaled)
    if near:
        parts = [high, high, middle, high, low, middle]
    else:
        parts = [high, middle, high, low, high, middle]
    return jnp.concatenate(parts + [tail.astype(BF16)], axis=0)


def kernel(
    n, ladder, points_ref, targets_ref, noise_ref, inv_ref, sol_ref, res_ref, dir_ref,
    held, near, total, mine, stats, send_sem, recv_sem, stat_send, stat_recv,
):
    features, count = points_ref.shape
    columns = targets_ref.shape[0]
    chips = n // 2
    half = chips // 2
    me = lax.axis_index("blk")
    core, chip = lax.rem(me, 2), lax.div(me, 2)

    if ladder:
        side, level = lax.rem(chip, 2), lax.div(chip, 2)
        place = level + side * (chips - 1 - 2 * level)
    else:
        place = chip

    def device_at(place):
        place = lax.rem(place + chips, chips)
        if ladder:
            side = lax.div(place, half)
            level = place + side * (chips - 1 - 2 * place)
            place = 2 * level + side
        return 2 * place + core

    toward = 1 - 2 * core
    ahead = device_at(place + toward)
    behind = device_at(place - toward)
    sibling = 2 * chip + 1 - core

    def copy(source, slot, target):
        return pltpu.make_async_remote_copy(
            src_ref=held.at[source],
            dst_ref=held.at[slot],
            send_sem=send_sem.at[slot],
            recv_sem=recv_sem.at[slot],
            device_id={"blk": target},
            device_id_type=pl.DeviceIdType.MESH,
        )

    def stat_copy(offset):
        return pltpu.make_async_remote_copy(
            src_ref=mine,
            dst_ref=stats.at[offset],
            send_sem=stat_send.at[offset],
            recv_sem=stat_recv.at[offset],
            device_id={"blk": lax.rem(me + offset, n)},
            device_id_type=pl.DeviceIdType.MESH,
        )

    barrier = pltpu.get_barrier_semaphore()

    def greet(offset, _):
        pl.semaphore_signal(
            barrier,
            inc=1,
            device_id={"blk": lax.rem(me + offset, n)},
            device_id_type=pl.DeviceIdType.MESH,
        )
        return 0

    lax.fori_loop(1, n, greet, 0)

    eye = lax.broadcasted_iota(jnp.int32, (features, features), 0) == lax.broadcasted_iota(
        jnp.int32, (features, features), 1
    )
    inv = jnp.sum(jnp.where(eye, inv_ref[...], 0.0), axis=1, keepdims=True)
    held[0, :features] = points_ref[...] * inv * (LOG2E**0.5)
    held[0, features:] = targets_ref[...]
    pl.semaphore_wait(barrier, n - 1)
    copy(0, 2, ahead).start()
    copy(0, 3, behind).start()
    copy(0, 1, sibling).start()
    near[...] = augmented(held[0, :features], True).astype(F32).T.astype(BF16)
    total[...] = jnp.zeros_like(total)

    def visit(slot, _):
        hop = lax.div(slot + 2, 4)
        phase = lax.rem(slot, 4)

        @pl.when(slot > 0)
        def _():
            @pl.when(jnp.logical_or(phase != 3, slot == n - 1))
            def _():
                copy(0, slot, sibling).wait_recv()

            @pl.when(phase == 2)
            def _():
                @pl.when(hop < half)
                def _():
                    copy(slot, slot + 4, ahead).start()
                    copy(slot, slot + 2, sibling).start()
                    copy(0, slot + 1, sibling).wait_recv()

                    @pl.when(hop < half - 1)
                    def _():
                        copy(slot + 1, slot + 5, behind).start()

                    copy(slot + 1, slot + 3, sibling).start()

                @pl.when(hop == half)
                def _():
                    copy(slot, slot + 1, sibling).start()

        block = held[slot]
        far = augmented(block[:features], False)
        vectors = block[features:]
        high = vectors.astype(BF16)
        low = (vectors - high.astype(F32)).astype(BF16)
        pair = jnp.concatenate([high, low], axis=0)
        exponent = jnp.dot(near[...], far, preferred_element_type=F32)
        values = jnp.exp2(exponent)
        upper = values.astype(BF16)
        lower = (values - upper.astype(F32)).astype(BF16)
        contract = (((1,), (1,)), ((), ()))
        total[...] += lax.dot_general(upper, pair, contract, preferred_element_type=F32) + (
            lax.dot_general(lower, pair, contract, preferred_element_type=F32)
        )
        return 0

    lax.fori_loop(0, n, visit, 0)

    summed = total[...].T
    targets = held[0, features:]
    image = summed[:columns] + summed[columns:] + noise_ref[...] * targets

    def over_points(value):
        return jnp.sum(value, axis=1, keepdims=True)

    curvature = over_points(targets * image)
    image_norm = over_points(image * image)
    best = jnp.where(image_norm > 0.0, curvature / jnp.where(image_norm > 0.0, image_norm, 1.0), 0.0)
    rest = targets - best * image
    lane = lax.broadcasted_iota(jnp.int32, mine.shape, 1)
    packed = jnp.zeros(mine.shape, F32)
    for index, value in enumerate(
        (curvature, over_points(targets * targets), over_points(rest * rest), image_norm, best)
    ):
        packed = jnp.where(lane == index, value, packed)
    mine[...] = packed
    stats[0] = packed

    def send(offset, _):
        stat_copy(offset).start()
        return 0

    def receive(offset, _):
        stat_copy(offset).wait_recv()
        return 0

    lax.fori_loop(1, n, send, 0)
    lax.fori_loop(1, n, receive, 0)

    def add(offset, state):
        return state + stats[offset]

    sums = lax.fori_loop(0, n, add, jnp.zeros(mine.shape, F32), unroll=True)
    norm_now = sums[:, 1:2]
    step_size = norm_now / sums[:, 0:1]

    def add_norm(offset, state):
        part = stats[offset]
        gap = step_size - part[:, 4:5]
        return state + (part[:, 2:3] + gap * gap * part[:, 3:4])

    norm_next = lax.fori_loop(0, n, add_norm, jnp.zeros((columns, 1), F32), unroll=True)
    residual = targets - step_size * image
    sol_ref[...] = step_size * targets
    res_ref[...] = residual
    dir_ref[...] = residual + (norm_next / norm_now) * targets

    def finish(slot, _):
        copy(0, slot, sibling).wait_send()
        stat_copy(slot).wait_send()
        return 0

    lax.fori_loop(1, n, finish, 0)


def solution(mesh):
    n = mesh.shape["blk"]
    ladder = mesh.shape["groups"] == 2

    def body(points, targets, noise_var, inv_length):
        count, features = points.shape
        columns = targets.shape[1]
        out = jax.ShapeDtypeStruct((columns, count), F32)
        vmem = pl.BlockSpec(memory_space=pltpu.VMEM)
        outs = pl.pallas_call(
            functools.partial(kernel, n, ladder),
            out_shape=[out] * 3,
            in_specs=[vmem] * 4,
            out_specs=[vmem] * 3,
            scratch_shapes=[
                pltpu.VMEM((n, features + columns, count), F32),
                pltpu.VMEM((count, 6 * features + 16), BF16),
                pltpu.VMEM((count, 2 * columns), F32),
                pltpu.VMEM((columns, 128), F32),
                pltpu.VMEM((n, columns, 128), F32),
                pltpu.SemaphoreType.DMA((n,)),
                pltpu.SemaphoreType.DMA((n,)),
                pltpu.SemaphoreType.DMA((n,)),
                pltpu.SemaphoreType.DMA((n,)),
            ],
            compiler_params=pltpu.CompilerParams(
                collective_id=0, has_side_effects=True, vmem_limit_bytes=40 * 2**20
            ),
        )(points.T, targets.T, noise_var[None, :], inv_length[None, :])
        return tuple(value.T for value in outs)

    rows, flat = P(("groups", "blk"), None), P(("groups", "blk"))
    return jax.shard_map(
        body,
        mesh=mesh,
        in_specs=(rows, rows, flat, P()),
        out_specs=(rows,) * 3,
        check_vma=False,
    )
```

```python
import functools

import jax
import jax.numpy as jnp
from jax import lax
from jax.experimental import pallas as pl
from jax.experimental.pallas import tpu as pltpu
from jax.sharding import PartitionSpec as P

F32 = jnp.float32
BF16 = jnp.bfloat16
LOG2E = 1.4426950408889634


def split3(value):
    high = value.astype(BF16)
    rest = value - high.astype(F32)
    middle = rest.astype(BF16)
    low = (rest - middle.astype(F32)).astype(BF16)
    return high, middle, low


def augmented(scaled, near):
    count = scaled.shape[1]
    norm = -0.5 * jnp.sum(scaled * scaled, axis=0, keepdims=True)
    row = lax.broadcasted_iota(jnp.int32, (16, count), 0)
    first = 0 if near else 3
    tail = jnp.where(row < 6, 1.0, 0.0)
    for offset, part in enumerate(split3(norm)):
        spread = jnp.broadcast_to(part.astype(F32), (16, count))
        tail = jnp.where(row == first + offset, spread, tail)
    high, middle, low = split3(scaled)
    if near:
        parts = [high, high, middle, high, low, middle]
    else:
        parts = [high, middle, high, low, high, middle]
    return jnp.concatenate(parts + [tail.astype(BF16)], axis=0)


def kernel(
    n, ladder, points_ref, targets_ref, noise_ref, inv_ref, sol_ref, res_ref, dir_ref,
    held, points, noise, inverse, near, total, mine, layer, line,
    send_sem, recv_sem, load_sem, layer_send, layer_recv, line_send, line_recv,
):
    features, count = points_ref.shape
    columns = targets_ref.shape[0]
    width = count // 2
    chips = n // 2
    half = chips // 2
    last = n - 2
    quads = n // 4
    me = lax.axis_index("blk")
    core, chip = lax.rem(me, 2), lax.div(me, 2)
    corner, quad = lax.rem(me, 4), lax.div(me, 4)

    if ladder:
        side, level = lax.rem(chip, 2), lax.div(chip, 2)
        place = level + side * (chips - 1 - 2 * level)
    else:
        place = chip

    def device_at(place):
        place = lax.rem(place + chips, chips)
        if ladder:
            side = lax.div(place, half)
            level = place + side * (chips - 1 - 2 * place)
            place = 2 * level + side
        return 2 * place + core

    toward = 1 - 2 * core
    ahead = device_at(place + toward)
    behind = device_at(place - toward)
    sibling = 2 * chip + 1 - core
    layer_peers = [4 * quad + lax.rem(corner + offset, 4) for offset in range(1, 4)]
    line_peers = [4 * lax.rem(quad + offset, quads) + corner for offset in range(1, quads)]

    def remote(source, target_ref, sent, received, target):
        return pltpu.make_async_remote_copy(
            src_ref=source,
            dst_ref=target_ref,
            send_sem=sent,
            recv_sem=received,
            device_id={"blk": target},
            device_id_type=pl.DeviceIdType.MESH,
        )

    def chunk(unit, part, to_unit, to_part, target):
        index = 2 * to_unit + to_part
        return remote(
            held.at[unit, part], held.at[to_unit, to_part], send_sem.at[index], recv_sem.at[index], target
        )

    def share(unit, to_unit):
        index = 2 * to_unit
        return remote(held.at[unit], held.at[to_unit], send_sem.at[index], recv_sem.at[index], sibling)

    barrier = pltpu.get_barrier_semaphore()
    friends = layer_peers + line_peers
    if not ladder:
        friends = friends + [ahead, behind]
    for friend in friends:
        pl.semaphore_signal(
            barrier, inc=1, device_id={"blk": friend}, device_id_type=pl.DeviceIdType.MESH
        )

    loads = [
        pltpu.make_async_copy(points_ref, points, load_sem.at[0]),
        pltpu.make_async_copy(
            targets_ref.at[:, :width], held.at[0, 0, features:], load_sem.at[1]
        ),
        pltpu.make_async_copy(
            targets_ref.at[:, width:], held.at[0, 1, features:], load_sem.at[2]
        ),
        pltpu.make_async_copy(inv_ref, inverse, load_sem.at[3]),
        pltpu.make_async_copy(noise_ref, noise, load_sem.at[4]),
    ]
    for load in loads:
        load.start()
    total[...] = jnp.zeros_like(total)
    for load in loads:
        load.wait()

    eye = lax.broadcasted_iota(jnp.int32, (features, features), 0) == lax.broadcasted_iota(
        jnp.int32, (features, features), 1
    )
    inv = jnp.sum(jnp.where(eye, inverse[...], 0.0), axis=1, keepdims=True)
    scaled = points[...] * inv * (LOG2E**0.5)
    held[0, 0, :features] = scaled[:, :width]
    held[0, 1, :features] = scaled[:, width:]
    pl.semaphore_wait(barrier, len(friends))
    for part in range(2):
        chunk(0, part, 2 + part, 0, ahead).start()
        chunk(0, part, 2 + part, 1, behind).start()
    share(0, 1).start()
    near[...] = augmented(scaled, True).astype(F32).T.astype(BF16)

    def visit(unit, _):
        hop = lax.div(unit + 2, 4)
        phase = lax.rem(unit + 2, 4)
        ring = jnp.logical_and(jnp.logical_and(phase < 2, unit > 0), unit < n - 1)

        @pl.when(jnp.logical_and(unit > 0, jnp.logical_not(ring)))
        def _():
            share(0, unit).wait_recv()

        @pl.when(ring)
        def _():
            chunk(0, 0, unit, 0, sibling).wait_recv()

            @pl.when(hop < half - 1)
            def _():
                chunk(unit, 0, unit + 4, 0, ahead).start()

            @pl.when(hop == half - 1)
            def _():
                chunk(unit, 0, last, phase, ahead).start()

            chunk(0, 0, unit, 1, sibling).wait_recv()

            @pl.when(hop < half - 1)
            def _():
                chunk(unit, 1, unit + 4, 1, behind).start()

            @pl.when(hop < half)
            def _():
                share(unit, unit + 2).start()

            @pl.when(hop == half)
            def _():
                share(unit, unit + 1).start()

        block = jnp.concatenate([held[unit, 0], held[unit, 1]], axis=1)
        far = augmented(block[:features], False)
        vectors = block[features:]
        high = vectors.astype(BF16)
        low = (vectors - high.astype(F32)).astype(BF16)
        pair = jnp.concatenate([high, low], axis=0)
        exponent = jnp.dot(near[...], far, preferred_element_type=F32)
        values = jnp.exp2(exponent)
        upper = values.astype(BF16)
        lower = (values - upper.astype(F32)).astype(BF16)
        contract = (((1,), (1,)), ((), ()))
        total[...] += lax.dot_general(upper, pair, contract, preferred_element_type=F32) + (
            lax.dot_general(lower, pair, contract, preferred_element_type=F32)
        )
        return 0

    lax.fori_loop(0, n, visit, 0)

    summed = total[...].T
    targets = jnp.concatenate([held[0, 0, features:], held[0, 1, features:]], axis=1)
    image = summed[:columns] + summed[columns:] + noise[...] * targets

    def over_points(value):
        return jnp.sum(value, axis=1, keepdims=True)

    def quotient(top, bottom):
        return jnp.where(bottom > 0.0, top / jnp.where(bottom > 0.0, bottom, 1.0), 0.0)

    lane = lax.broadcasted_iota(jnp.int32, mine.shape, 1)

    def packed(*values):
        result = jnp.zeros(mine.shape, F32)
        for index, value in enumerate(values):
            result = jnp.where(lane == index, value, result)
        return result

    def unpacked(value):
        return [jnp.broadcast_to(value[:, i : i + 1], mine.shape) for i in range(5)]

    def rests_at(step, parts):
        rests = 0.0
        for part in parts:
            gap = step - part[4]
            rests += part[2] + gap * gap * part[3]
        return rests

    def exchange(box, sent, received, peers):
        copies = [
            remote(box.at[0], box.at[offset], sent.at[offset], received.at[offset], peer)
            for offset, peer in enumerate(peers, 1)
        ]
        for copy in copies:
            copy.start()
        for copy in copies:
            copy.wait_recv()
        return copies, [unpacked(box[offset]) for offset in range(len(peers) + 1)]

    curvature = over_points(targets * image)
    image_norm = over_points(image * image)
    best = quotient(curvature, image_norm)
    rest = targets - best * image
    layer[0] = packed(
        curvature, over_points(targets * targets), over_points(rest * rest), image_norm, best
    )
    layer_copies, parts = exchange(layer, layer_send, layer_recv, layer_peers)
    curvature, norm_now, image_norm = [sum(part[i] for part in parts) for i in (0, 1, 3)]
    best = quotient(curvature, image_norm)
    line[0] = packed(curvature, norm_now, rests_at(best, parts), image_norm, best)
    line_copies, parts = exchange(line, line_send, line_recv, line_peers)
    curvature, norm_now = [sum(part[i] for part in parts) for i in (0, 1)]
    step_size = norm_now / curvature
    ratio = (rests_at(step_size, parts) / norm_now)[:, :1]
    step_size = step_size[:, :1]
    residual = targets - step_size * image
    sol_ref[...] = step_size * targets
    res_ref[...] = residual
    dir_ref[...] = residual + ratio * targets

    def finish(unit, _):
        phase = lax.rem(unit + 2, 4)
        ring = jnp.logical_and(phase < 2, unit < n - 1)

        @pl.when(ring)
        def _():
            chunk(0, 0, unit, 0, sibling).wait_send()
            chunk(0, 0, unit, 1, sibling).wait_send()

        @pl.when(jnp.logical_not(ring))
        def _():
            share(0, unit).wait_send()

        return 0

    lax.fori_loop(1, n, finish, 0)
    for copy in layer_copies + line_copies:
        copy.wait_send()


def solution(mesh):
    n = mesh.shape["blk"]
    ladder = mesh.shape["groups"] == 2

    def body(points, targets, noise_var, inv_length):
        count, features = points.shape
        columns = targets.shape[1]
        out = jax.ShapeDtypeStruct((columns, count), F32)
        outs = pl.pallas_call(
            functools.partial(kernel, n, ladder),
            out_shape=[out] * 3,
            in_specs=[pl.BlockSpec(memory_space=pl.ANY)] * 4,
            out_specs=[pl.BlockSpec(memory_space=pltpu.VMEM)] * 3,
            scratch_shapes=[
                pltpu.VMEM((n, 2, features + columns, count // 2), F32),
                pltpu.VMEM((features, count), F32),
                pltpu.VMEM((1, count), F32),
                pltpu.VMEM((1, features), F32),
                pltpu.VMEM((count, 6 * features + 16), BF16),
                pltpu.VMEM((count, 2 * columns), F32),
                pltpu.VMEM((columns, 128), F32),
                pltpu.VMEM((4, columns, 128), F32),
                pltpu.VMEM((n // 4, columns, 128), F32),
                pltpu.SemaphoreType.DMA((2 * n,)),
                pltpu.SemaphoreType.DMA((2 * n,)),
                pltpu.SemaphoreType.DMA((5,)),
                pltpu.SemaphoreType.DMA((4,)),
                pltpu.SemaphoreType.DMA((4,)),
                pltpu.SemaphoreType.DMA((n // 4,)),
                pltpu.SemaphoreType.DMA((n // 4,)),
            ],
            compiler_params=pltpu.CompilerParams(collective_id=0, has_side_effects=True),
        )(points.T, targets.T, noise_var[None, :], inv_length[None, :])
        return tuple(value.T for value in outs)

    rows, flat = P(("groups", "blk"), None), P(("groups", "blk"))
    return jax.shard_map(
        body,
        mesh=mesh,
        in_specs=(rows, rows, flat, P()),
        out_specs=(rows,) * 3,
        check_vma=False,
    )
```

```python
import functools

import jax
import jax.numpy as jnp
from jax import lax
from jax.experimental import pallas as pl
from jax.experimental.pallas import tpu as pltpu
from jax.sharding import PartitionSpec as P

F32 = jnp.float32
BF16 = jnp.bfloat16
LOG2E = 1.4426950408889634


def split3(value):
    high = value.astype(BF16)
    rest = value - high.astype(F32)
    middle = rest.astype(BF16)
    low = (rest - middle.astype(F32)).astype(BF16)
    return high, middle, low


def augmented(scaled, near):
    count = scaled.shape[1]
    norm = -0.5 * jnp.sum(scaled * scaled, axis=0, keepdims=True)
    row = lax.broadcasted_iota(jnp.int32, (16, count), 0)
    first = 0 if near else 3
    tail = jnp.where(row < 6, 1.0, 0.0)
    for offset, part in enumerate(split3(norm)):
        spread = jnp.broadcast_to(part.astype(F32), (16, count))
        tail = jnp.where(row == first + offset, spread, tail)
    high, middle, low = split3(scaled)
    if near:
        parts = [high, high, middle, high, low, middle]
    else:
        parts = [high, middle, high, low, high, middle]
    return jnp.concatenate(parts + [tail.astype(BF16)], axis=0)


def kernel(
    n, ladder, points_ref, targets_ref, noise_ref, inv_ref, out_ref,
    held, points, noise, inverse, near, total, stats,
    send_sem, recv_sem, load_sem, stat_send, stat_recv,
):
    features, count = points_ref.shape
    columns = targets_ref.shape[0]
    width = count // 2
    chips = n // 2
    half = chips // 2
    last = n - 2
    me = lax.axis_index("blk")
    core, chip = lax.rem(me, 2), lax.div(me, 2)

    if ladder:
        side, level = lax.rem(chip, 2), lax.div(chip, 2)
        place = level + side * (chips - 1 - 2 * level)
    else:
        place = chip

    def device_at(place):
        place = lax.rem(place + chips, chips)
        if ladder:
            side = lax.div(place, half)
            level = place + side * (chips - 1 - 2 * place)
            place = 2 * level + side
        return 2 * place + core

    toward = 1 - 2 * core
    ahead = device_at(place + toward)
    behind = device_at(place - toward)
    sibling = 2 * chip + 1 - core

    def remote(source, target_ref, sent, received, target):
        return pltpu.make_async_remote_copy(
            src_ref=source,
            dst_ref=target_ref,
            send_sem=sent,
            recv_sem=received,
            device_id={"blk": target},
            device_id_type=pl.DeviceIdType.MESH,
        )

    def chunk(unit, part, to_unit, to_part, target):
        index = 2 * to_unit + to_part
        return remote(
            held.at[unit, part], held.at[to_unit, to_part], send_sem.at[index], recv_sem.at[index], target
        )

    def share(unit, to_unit):
        index = 2 * to_unit
        return remote(held.at[unit], held.at[to_unit], send_sem.at[index], recv_sem.at[index], sibling)

    barrier = pltpu.get_barrier_semaphore()
    friends = [ahead, behind, sibling]
    for friend in friends:
        pl.semaphore_signal(
            barrier, inc=1, device_id={"blk": friend}, device_id_type=pl.DeviceIdType.MESH
        )

    loads = [
        pltpu.make_async_copy(points_ref, points, load_sem.at[0]),
        pltpu.make_async_copy(
            targets_ref.at[:, :width], held.at[0, 0, features:], load_sem.at[1]
        ),
        pltpu.make_async_copy(
            targets_ref.at[:, width:], held.at[0, 1, features:], load_sem.at[2]
        ),
        pltpu.make_async_copy(inv_ref, inverse, load_sem.at[3]),
        pltpu.make_async_copy(noise_ref, noise, load_sem.at[4]),
    ]
    for load in loads:
        load.start()
    total[...] = jnp.zeros_like(total)
    for load in loads:
        load.wait()

    eye = lax.broadcasted_iota(jnp.int32, (features, features), 0) == lax.broadcasted_iota(
        jnp.int32, (features, features), 1
    )
    inv = jnp.sum(jnp.where(eye, inverse[...], 0.0), axis=1, keepdims=True)
    scaled = points[...] * inv * (LOG2E**0.5)
    held[0, 0, :features] = scaled[:, :width]
    held[0, 1, :features] = scaled[:, width:]
    pl.semaphore_wait(barrier, len(friends))
    chunk(0, 0, 2, 0, ahead).start()
    chunk(0, 0, 2, 1, behind).start()
    share(0, 1).start()
    near[...] = augmented(scaled, True).astype(F32).T.astype(BF16)

    def visit(unit, _):
        hop = lax.div(unit + 2, 4)
        phase = lax.rem(unit + 2, 4)
        ring = jnp.logical_and(jnp.logical_and(phase < 2, unit > 0), unit < n - 1)

        @pl.when(unit == 1)
        def _():
            chunk(0, 1, 3, 0, ahead).start()
            chunk(0, 1, 3, 1, behind).start()

        @pl.when(jnp.logical_and(unit > 0, jnp.logical_not(ring)))
        def _():
            share(0, unit).wait_recv()

        @pl.when(ring)
        def _():
            chunk(0, 0, unit, 0, sibling).wait_recv()

            @pl.when(hop < half - 1)
            def _():
                chunk(unit, 0, unit + 4, 0, ahead).start()

            @pl.when(hop == half - 1)
            def _():
                chunk(unit, 0, last, phase, ahead).start()

            chunk(0, 0, unit, 1, sibling).wait_recv()

            @pl.when(hop < half - 1)
            def _():
                chunk(unit, 1, unit + 4, 1, behind).start()

            @pl.when(hop < half)
            def _():
                share(unit, unit + 2).start()

            @pl.when(hop == half)
            def _():
                share(unit, unit + 1).start()

        block = jnp.concatenate([held[unit, 0], held[unit, 1]], axis=1)
        far = augmented(block[:features], False)
        vectors = block[features:]
        high = vectors.astype(BF16)
        low = (vectors - high.astype(F32)).astype(BF16)
        pair = jnp.concatenate([high, low], axis=0)
        exponent = jnp.dot(near[...], far, preferred_element_type=F32)
        values = jnp.exp2(exponent)
        upper = values.astype(BF16)
        lower = (values - upper.astype(F32)).astype(BF16)
        contract = (((1,), (1,)), ((), ()))
        total[...] += lax.dot_general(upper, pair, contract, preferred_element_type=F32) + (
            lax.dot_general(lower, pair, contract, preferred_element_type=F32)
        )
        return 0

    lax.fori_loop(0, n, visit, 0)

    summed = total[...].T
    targets = jnp.concatenate([held[0, 0, features:], held[0, 1, features:]], axis=1)
    image = summed[:columns] + summed[columns:] + noise[...] * targets

    def over_points(value):
        return jnp.sum(value, axis=1, keepdims=True)

    def quotient(top, bottom):
        return jnp.where(bottom > 0.0, top / jnp.where(bottom > 0.0, bottom, 1.0), 0.0)

    shape = stats.shape[1:]
    lane = lax.broadcasted_iota(jnp.int32, shape, 1)

    def packed(*values):
        result = jnp.zeros(shape, F32)
        for index, value in enumerate(values):
            result = jnp.where(lane == index, value, result)
        return result

    def unpacked(value):
        return [jnp.broadcast_to(value[:, i : i + 1], shape) for i in range(5)]

    def stat_copy(offset):
        return remote(
            stats.at[0], stats.at[offset], stat_send.at[offset], stat_recv.at[offset], lax.rem(me + offset, n)
        )

    def stat_start(offset, _):
        stat_copy(offset).start()
        return 0

    def stat_wait(offset, _):
        stat_copy(offset).wait_recv()
        return 0

    curvature = over_points(targets * image)
    image_norm = over_points(image * image)
    best = quotient(curvature, image_norm)
    rest = targets - best * image
    stats[0] = packed(
        curvature, over_points(targets * targets), over_points(rest * rest), image_norm, best
    )
    lax.fori_loop(1, n, stat_start, 0)
    lax.fori_loop(1, n, stat_wait, 0)
    parts = [stats[offset] for offset in range(n)]
    sums = sum(parts)
    norm_now = sums[:, 1:2]
    step_size = norm_now / sums[:, :1]
    wide_step = jnp.broadcast_to(step_size, shape)
    rests = 0.0
    for part in parts:
        gap = wide_step - jnp.broadcast_to(part[:, 4:5], shape)
        rests += part + gap * gap * jnp.broadcast_to(part[:, 3:4], shape)
    ratio = rests[:, 2:3] / norm_now
    residual = targets - step_size * image
    out_ref[:columns] = step_size * targets
    out_ref[columns : 2 * columns] = residual
    out_ref[2 * columns :] = residual + ratio * targets

    def finish(unit, _):
        phase = lax.rem(unit + 2, 4)
        ring = jnp.logical_and(phase < 2, unit < n - 1)

        @pl.when(ring)
        def _():
            chunk(0, 0, unit, 0, sibling).wait_send()
            chunk(0, 0, unit, 1, sibling).wait_send()

        @pl.when(jnp.logical_not(ring))
        def _():
            share(0, unit).wait_send()

        return 0

    lax.fori_loop(1, n, finish, 0)

    def stat_finish(offset, _):
        stat_copy(offset).wait_send()
        return 0

    lax.fori_loop(1, n, stat_finish, 0)


def spread(packed_ref, sol_ref, res_ref, dir_ref, sem):
    columns = sol_ref.shape[0]
    copies = [
        pltpu.make_async_copy(packed_ref.at[pl.ds(i * columns, columns)], ref, sem.at[i])
        for i, ref in enumerate((sol_ref, res_ref, dir_ref))
    ]
    for copy in copies:
        copy.start()
    for copy in copies:
        copy.wait()


def solution(mesh):
    n = mesh.shape["blk"]
    ladder = mesh.shape["groups"] == 2

    def body(points, targets, noise_var, inv_length):
        count, features = points.shape
        columns = targets.shape[1]
        out = jax.ShapeDtypeStruct((columns, count), F32)
        packed = pl.pallas_call(
            functools.partial(kernel, n, ladder),
            out_shape=jax.ShapeDtypeStruct((3 * columns, count), F32),
            in_specs=[pl.BlockSpec(memory_space=pl.ANY)] * 4,
            out_specs=pl.BlockSpec(memory_space=pltpu.VMEM),
            scratch_shapes=[
                pltpu.VMEM((n, 2, features + columns, count // 2), F32),
                pltpu.VMEM((features, count), F32),
                pltpu.VMEM((1, count), F32),
                pltpu.VMEM((1, features), F32),
                pltpu.VMEM((count, 6 * features + 16), BF16),
                pltpu.VMEM((count, 2 * columns), F32),
                pltpu.VMEM((n, columns, 128), F32),
                pltpu.SemaphoreType.DMA((2 * n,)),
                pltpu.SemaphoreType.DMA((2 * n,)),
                pltpu.SemaphoreType.DMA((5,)),
                pltpu.SemaphoreType.DMA((n,)),
                pltpu.SemaphoreType.DMA((n,)),
            ],
            compiler_params=pltpu.CompilerParams(collective_id=0, has_side_effects=True),
        )(points.T, targets.T, noise_var[None, :], inv_length[None, :])
        outs = pl.pallas_call(
            spread,
            out_shape=[out] * 3,
            in_specs=[pl.BlockSpec(memory_space=pltpu.VMEM)],
            out_specs=[pl.BlockSpec(memory_space=pl.ANY)] * 3,
            scratch_shapes=[pltpu.SemaphoreType.DMA((3,))],
        )(packed)
        return tuple(value.T for value in outs)

    rows, flat = P(("groups", "blk"), None), P(("groups", "blk"))
    return jax.shard_map(
        body,
        mesh=mesh,
        in_specs=(rows, rows, flat, P()),
        out_specs=(rows,) * 3,
        check_vma=False,
    )
```

```python
import functools

import jax
import jax.numpy as jnp
from jax import lax
from jax.experimental import pallas as pl
from jax.experimental.pallas import tpu as pltpu
from jax.sharding import PartitionSpec as P

F32 = jnp.float32
BF16 = jnp.bfloat16
LOG2E = 1.4426950408889634


def split3(value):
    high = value.astype(BF16)
    rest = value - high.astype(F32)
    middle = rest.astype(BF16)
    low = (rest - middle.astype(F32)).astype(BF16)
    return high, middle, low


def augmented(scaled, near):
    count = scaled.shape[1]
    norm = -0.5 * jnp.sum(scaled * scaled, axis=0, keepdims=True)
    row = lax.broadcasted_iota(jnp.int32, (16, count), 0)
    first = 0 if near else 3
    tail = jnp.where(row < 6, 1.0, 0.0)
    for offset, part in enumerate(split3(norm)):
        spread = jnp.broadcast_to(part.astype(F32), (16, count))
        tail = jnp.where(row == first + offset, spread, tail)
    high, middle, low = split3(scaled)
    if near:
        parts = [high, high, middle, high, low, middle]
    else:
        parts = [high, middle, high, low, high, middle]
    return jnp.concatenate(parts + [tail.astype(BF16)], axis=0)


def kernel(
    n, ladder, points_ref, targets_ref, noise_ref, inv_ref, out_ref,
    held, points, noise, inverse, near, total, stats,
    send_sem, recv_sem, load_sem, stat_send, stat_recv,
):
    features, count = points_ref.shape
    columns = targets_ref.shape[0]
    width = count // 2
    chips = n // 2
    half = chips // 2
    last = n - 2
    me = lax.axis_index("blk")
    core, chip = lax.rem(me, 2), lax.div(me, 2)

    if ladder:
        side, level = lax.rem(chip, 2), lax.div(chip, 2)
        place = level + side * (chips - 1 - 2 * level)
    else:
        place = chip

    def device_at(place):
        place = lax.rem(place + chips, chips)
        if ladder:
            side = lax.div(place, half)
            level = place + side * (chips - 1 - 2 * place)
            place = 2 * level + side
        return 2 * place + core

    toward = 1 - 2 * core
    ahead = device_at(place + toward)
    behind = device_at(place - toward)
    opposite = device_at(place + half)
    sibling = 2 * chip + 1 - core

    def remote(source, target_ref, sent, received, target):
        return pltpu.make_async_remote_copy(
            src_ref=source,
            dst_ref=target_ref,
            send_sem=sent,
            recv_sem=received,
            device_id={"blk": target},
            device_id_type=pl.DeviceIdType.MESH,
        )

    def chunk(unit, part, to_unit, to_part, target):
        index = 2 * to_unit + to_part
        return remote(
            held.at[unit, part], held.at[to_unit, to_part], send_sem.at[index], recv_sem.at[index], target
        )

    def share(unit, to_unit):
        index = 2 * to_unit
        return remote(held.at[unit], held.at[to_unit], send_sem.at[index], recv_sem.at[index], sibling)

    barrier = pltpu.get_barrier_semaphore()
    friends = [ahead, behind, sibling, opposite]
    for friend in friends:
        pl.semaphore_signal(
            barrier, inc=1, device_id={"blk": friend}, device_id_type=pl.DeviceIdType.MESH
        )

    loads = [
        pltpu.make_async_copy(points_ref, points, load_sem.at[0]),
        pltpu.make_async_copy(
            targets_ref.at[:, :width], held.at[0, 0, features:], load_sem.at[1]
        ),
        pltpu.make_async_copy(
            targets_ref.at[:, width:], held.at[0, 1, features:], load_sem.at[2]
        ),
        pltpu.make_async_copy(inv_ref, inverse, load_sem.at[3]),
        pltpu.make_async_copy(noise_ref, noise, load_sem.at[4]),
    ]
    for load in loads:
        load.start()
    total[...] = jnp.zeros_like(total)
    for load in loads:
        load.wait()

    eye = lax.broadcasted_iota(jnp.int32, (features, features), 0) == lax.broadcasted_iota(
        jnp.int32, (features, features), 1
    )
    inv = jnp.sum(jnp.where(eye, inverse[...], 0.0), axis=1, keepdims=True)
    scaled = points[...] * inv * (LOG2E**0.5)
    held[0, 0, :features] = scaled[:, :width]
    held[0, 1, :features] = scaled[:, width:]
    pl.semaphore_wait(barrier, len(friends))
    chunk(0, 0, 2, 0, ahead).start()
    chunk(0, 0, 2, 1, behind).start()
    share(0, 1).start()
    near[...] = augmented(scaled, True).astype(F32).T.astype(BF16)

    def visit(unit, _):
        hop = lax.div(unit + 2, 4)
        phase = lax.rem(unit + 2, 4)
        ring = jnp.logical_and(jnp.logical_and(phase < 2, unit > 0), unit < n - 1)

        @pl.when(unit == 1)
        def _():
            chunk(0, 1, 3, 0, ahead).start()
            chunk(0, 1, 3, 1, behind).start()

        @pl.when(jnp.logical_and(unit > 0, jnp.logical_not(ring)))
        def _():
            share(0, unit).wait_recv()

        @pl.when(ring)
        def _():
            chunk(0, 0, unit, 0, sibling).wait_recv()

            @pl.when(hop < half - 1)
            def _():
                chunk(unit, 0, unit + 4, 0, ahead).start()

            chunk(0, 0, unit, 1, sibling).wait_recv()

            @pl.when(hop < half - 1)
            def _():
                chunk(unit, 1, unit + 4, 1, behind).start()

            @pl.when(unit == 3)
            def _():
                chunk(0, 0, last, 0, opposite).start()
                chunk(0, 1, last, 1, opposite).start()

            @pl.when(hop < half)
            def _():
                share(unit, unit + 2).start()

            @pl.when(hop == half)
            def _():
                share(unit, unit + 1).start()

        block = jnp.concatenate([held[unit, 0], held[unit, 1]], axis=1)
        far = augmented(block[:features], False)
        vectors = block[features:]
        high = vectors.astype(BF16)
        low = (vectors - high.astype(F32)).astype(BF16)
        pair = jnp.concatenate([high, low], axis=0)
        exponent = jnp.dot(near[...], far, preferred_element_type=F32)
        values = jnp.exp2(exponent)
        upper = values.astype(BF16)
        lower = (values - upper.astype(F32)).astype(BF16)
        contract = (((1,), (1,)), ((), ()))
        total[...] += lax.dot_general(upper, pair, contract, preferred_element_type=F32) + (
            lax.dot_general(lower, pair, contract, preferred_element_type=F32)
        )
        return 0

    lax.fori_loop(0, n, visit, 0)

    summed = total[...].T
    targets = jnp.concatenate([held[0, 0, features:], held[0, 1, features:]], axis=1)
    image = summed[:columns] + summed[columns:] + noise[...] * targets

    def over_points(value):
        return jnp.sum(value, axis=1, keepdims=True)

    def quotient(top, bottom):
        return jnp.where(bottom > 0.0, top / jnp.where(bottom > 0.0, bottom, 1.0), 0.0)

    shape = stats.shape[1:]
    lane = lax.broadcasted_iota(jnp.int32, shape, 1)

    def packed(*values):
        result = jnp.zeros(shape, F32)
        for index, value in enumerate(values):
            result = jnp.where(lane == index, value, result)
        return result

    def unpacked(value):
        return [jnp.broadcast_to(value[:, i : i + 1], shape) for i in range(5)]

    def stat_copy(offset):
        return remote(
            stats.at[0], stats.at[offset], stat_send.at[offset], stat_recv.at[offset], lax.rem(me + offset, n)
        )

    def stat_start(offset, _):
        stat_copy(offset).start()
        return 0

    def stat_wait(offset, _):
        stat_copy(offset).wait_recv()
        return 0

    curvature = over_points(targets * image)
    image_norm = over_points(image * image)
    best = quotient(curvature, image_norm)
    rest = targets - best * image
    stats[0] = packed(
        curvature, over_points(targets * targets), over_points(rest * rest), image_norm, best
    )
    lax.fori_loop(1, n, stat_start, 0)
    lax.fori_loop(1, n, stat_wait, 0)
    parts = [stats[offset] for offset in range(n)]
    sums = sum(parts)
    norm_now = sums[:, 1:2]
    step_size = norm_now / sums[:, :1]
    wide_step = jnp.broadcast_to(step_size, shape)
    rests = 0.0
    for part in parts:
        gap = wide_step - jnp.broadcast_to(part[:, 4:5], shape)
        rests += part + gap * gap * jnp.broadcast_to(part[:, 3:4], shape)
    ratio = rests[:, 2:3] / norm_now
    residual = targets - step_size * image
    out_ref[:columns] = step_size * targets
    out_ref[columns : 2 * columns] = residual
    out_ref[2 * columns :] = residual + ratio * targets

    def finish(unit, _):
        phase = lax.rem(unit + 2, 4)
        ring = jnp.logical_and(phase < 2, unit < n - 1)

        @pl.when(ring)
        def _():
            chunk(0, 0, unit, 0, sibling).wait_send()
            chunk(0, 0, unit, 1, sibling).wait_send()

        @pl.when(jnp.logical_not(ring))
        def _():
            share(0, unit).wait_send()

        return 0

    lax.fori_loop(1, n, finish, 0)

    def stat_finish(offset, _):
        stat_copy(offset).wait_send()
        return 0

    lax.fori_loop(1, n, stat_finish, 0)


def spread(packed_ref, sol_ref, res_ref, dir_ref, sem):
    columns = sol_ref.shape[0]
    copies = [
        pltpu.make_async_copy(packed_ref.at[pl.ds(i * columns, columns)], ref, sem.at[i])
        for i, ref in enumerate((sol_ref, res_ref, dir_ref))
    ]
    for copy in copies:
        copy.start()
    for copy in copies:
        copy.wait()


def solution(mesh):
    n = mesh.shape["blk"]
    ladder = mesh.shape["groups"] == 2

    def body(points, targets, noise_var, inv_length):
        count, features = points.shape
        columns = targets.shape[1]
        out = jax.ShapeDtypeStruct((columns, count), F32)
        packed = pl.pallas_call(
            functools.partial(kernel, n, ladder),
            out_shape=jax.ShapeDtypeStruct((3 * columns, count), F32),
            in_specs=[pl.BlockSpec(memory_space=pl.ANY)] * 4,
            out_specs=pl.BlockSpec(memory_space=pltpu.VMEM),
            scratch_shapes=[
                pltpu.VMEM((n, 2, features + columns, count // 2), F32),
                pltpu.VMEM((features, count), F32),
                pltpu.VMEM((1, count), F32),
                pltpu.VMEM((1, features), F32),
                pltpu.VMEM((count, 6 * features + 16), BF16),
                pltpu.VMEM((count, 2 * columns), F32),
                pltpu.VMEM((n, columns, 128), F32),
                pltpu.SemaphoreType.DMA((2 * n,)),
                pltpu.SemaphoreType.DMA((2 * n,)),
                pltpu.SemaphoreType.DMA((5,)),
                pltpu.SemaphoreType.DMA((n,)),
                pltpu.SemaphoreType.DMA((n,)),
            ],
            compiler_params=pltpu.CompilerParams(collective_id=0, has_side_effects=True),
        )(points.T, targets.T, noise_var[None, :], inv_length[None, :])
        outs = pl.pallas_call(
            spread,
            out_shape=[out] * 3,
            in_specs=[pl.BlockSpec(memory_space=pltpu.VMEM)],
            out_specs=[pl.BlockSpec(memory_space=pl.ANY)] * 3,
            scratch_shapes=[pltpu.SemaphoreType.DMA((3,))],
        )(packed)
        return tuple(value.T for value in outs)

    rows, flat = P(("groups", "blk"), None), P(("groups", "blk"))
    return jax.shard_map(
        body,
        mesh=mesh,
        in_specs=(rows, rows, flat, P()),
        out_specs=(rows,) * 3,
        check_vma=False,
    )
```

```python
import functools

import jax
import jax.numpy as jnp
from jax import lax
from jax.experimental import pallas as pl
from jax.experimental.pallas import tpu as pltpu
from jax.sharding import PartitionSpec as P

F32 = jnp.float32
BF16 = jnp.bfloat16
LOG2E = 1.4426950408889634


def split3(value):
    high = value.astype(BF16)
    rest = value - high.astype(F32)
    middle = rest.astype(BF16)
    low = (rest - middle.astype(F32)).astype(BF16)
    return high, middle, low


def augmented(scaled, near):
    count = scaled.shape[1]
    norm = -0.5 * jnp.sum(scaled * scaled, axis=0, keepdims=True)
    row = lax.broadcasted_iota(jnp.int32, (16, count), 0)
    first = 0 if near else 3
    tail = jnp.where(row < 6, 1.0, 0.0)
    for offset, part in enumerate(split3(norm)):
        spread = jnp.broadcast_to(part.astype(F32), (16, count))
        tail = jnp.where(row == first + offset, spread, tail)
    high, middle, low = split3(scaled)
    if near:
        parts = [high, high, middle, high, low, middle]
    else:
        parts = [high, middle, high, low, high, middle]
    return jnp.concatenate(parts + [tail.astype(BF16)], axis=0)


def kernel(
    n, ladder, points_ref, targets_ref, noise_ref, inv_ref, out_ref,
    held, points, noise, inverse, near, total, stats,
    send_sem, recv_sem, load_sem, stat_send, stat_recv,
):
    features, count = points_ref.shape
    columns = targets_ref.shape[0]
    width = count // 2
    chips = n // 2
    half = chips // 2
    last = n - 2
    me = lax.axis_index("blk")
    core, chip = lax.rem(me, 2), lax.div(me, 2)

    if ladder:
        side, level = lax.rem(chip, 2), lax.div(chip, 2)
        place = level + side * (chips - 1 - 2 * level)
    else:
        place = chip

    def device_at(place):
        place = lax.rem(place + chips, chips)
        if ladder:
            side = lax.div(place, half)
            level = place + side * (chips - 1 - 2 * place)
            place = 2 * level + side
        return 2 * place + core

    toward = 1 - 2 * core
    ahead = device_at(place + toward)
    behind = device_at(place - toward)
    across = ahead + toward
    sibling = 2 * chip + 1 - core

    def remote(source, target_ref, sent, received, target):
        return pltpu.make_async_remote_copy(
            src_ref=source,
            dst_ref=target_ref,
            send_sem=sent,
            recv_sem=received,
            device_id={"blk": target},
            device_id_type=pl.DeviceIdType.MESH,
        )

    def chunk(unit, part, to_unit, to_part, target):
        index = 2 * to_unit + to_part
        return remote(
            held.at[unit, part], held.at[to_unit, to_part], send_sem.at[index], recv_sem.at[index], target
        )

    def share(unit, to_unit):
        index = 2 * to_unit
        return remote(held.at[unit], held.at[to_unit], send_sem.at[index], recv_sem.at[index], sibling)

    barrier = pltpu.get_barrier_semaphore()
    friends = [ahead, behind, sibling]
    for friend in friends:
        pl.semaphore_signal(
            barrier, inc=1, device_id={"blk": friend}, device_id_type=pl.DeviceIdType.MESH
        )

    loads = [
        pltpu.make_async_copy(points_ref, points, load_sem.at[0]),
        pltpu.make_async_copy(
            targets_ref.at[:, :width], held.at[0, 0, features:], load_sem.at[1]
        ),
        pltpu.make_async_copy(
            targets_ref.at[:, width:], held.at[0, 1, features:], load_sem.at[2]
        ),
        pltpu.make_async_copy(inv_ref, inverse, load_sem.at[3]),
        pltpu.make_async_copy(noise_ref, noise, load_sem.at[4]),
    ]
    for load in loads:
        load.start()
    total[...] = jnp.zeros_like(total)
    for load in loads:
        load.wait()

    eye = lax.broadcasted_iota(jnp.int32, (features, features), 0) == lax.broadcasted_iota(
        jnp.int32, (features, features), 1
    )
    inv = jnp.sum(jnp.where(eye, inverse[...], 0.0), axis=1, keepdims=True)
    scaled = points[...] * inv * (LOG2E**0.5)
    held[0, 0, :features] = scaled[:, :width]
    held[0, 1, :features] = scaled[:, width:]
    pl.semaphore_wait(barrier, len(friends))
    chunk(0, 0, 2, 0, ahead).start()
    chunk(0, 0, 2, 1, behind).start()
    chunk(0, 1, 3, 0, ahead).start()
    chunk(0, 1, 3, 1, behind).start()
    share(0, 1).start()
    near[...] = augmented(scaled, True).astype(F32).T.astype(BF16)

    def visit(unit, _):
        hop = lax.div(unit + 2, 4)
        phase = lax.rem(unit + 2, 4)
        ring = jnp.logical_and(phase < 2, unit > 0)

        @pl.when(jnp.logical_and(unit > 0, jnp.logical_not(ring)))
        def _():
            share(0, unit).wait_recv()

        @pl.when(ring)
        def _():
            chunk(0, 0, unit, 0, sibling).wait_recv()

            @pl.when(hop < half - 1)
            def _():
                chunk(unit, 0, unit + 4, 0, ahead).start()

            @pl.when(hop == half - 1)
            def _():
                chunk(unit, 0, last, phase, ahead).start()
                chunk(unit, 0, n - 1, phase, across).start()

            chunk(0, 0, unit, 1, sibling).wait_recv()

            @pl.when(hop < half - 1)
            def _():
                chunk(unit, 1, unit + 4, 1, behind).start()

            @pl.when(hop < half)
            def _():
                share(unit, unit + 2).start()

        block = jnp.concatenate([held[unit, 0], held[unit, 1]], axis=1)
        far = augmented(block[:features], False)
        vectors = block[features:]
        high = vectors.astype(BF16)
        low = (vectors - high.astype(F32)).astype(BF16)
        pair = jnp.concatenate([high, low], axis=0)
        exponent = jnp.dot(near[...], far, preferred_element_type=F32)
        values = jnp.exp2(exponent)
        upper = values.astype(BF16)
        lower = (values - upper.astype(F32)).astype(BF16)
        contract = (((1,), (1,)), ((), ()))
        total[...] += lax.dot_general(upper, pair, contract, preferred_element_type=F32) + (
            lax.dot_general(lower, pair, contract, preferred_element_type=F32)
        )
        return 0

    lax.fori_loop(0, n, visit, 0)

    summed = total[...].T
    targets = jnp.concatenate([held[0, 0, features:], held[0, 1, features:]], axis=1)
    image = summed[:columns] + summed[columns:] + noise[...] * targets

    def over_points(value):
        return jnp.sum(value, axis=1, keepdims=True)

    def quotient(top, bottom):
        return jnp.where(bottom > 0.0, top / jnp.where(bottom > 0.0, bottom, 1.0), 0.0)

    shape = stats.shape[1:]
    lane = lax.broadcasted_iota(jnp.int32, shape, 1)

    def packed(*values):
        result = jnp.zeros(shape, F32)
        for index, value in enumerate(values):
            result = jnp.where(lane == index, value, result)
        return result

    def unpacked(value):
        return [jnp.broadcast_to(value[:, i : i + 1], shape) for i in range(5)]

    def stat_copy(offset):
        return remote(
            stats.at[0], stats.at[offset], stat_send.at[offset], stat_recv.at[offset], lax.rem(me + offset, n)
        )

    def stat_start(offset, _):
        stat_copy(offset).start()
        return 0

    def stat_wait(offset, _):
        stat_copy(offset).wait_recv()
        return 0

    curvature = over_points(targets * image)
    image_norm = over_points(image * image)
    best = quotient(curvature, image_norm)
    rest = targets - best * image
    stats[0] = packed(
        curvature, over_points(targets * targets), over_points(rest * rest), image_norm, best
    )
    lax.fori_loop(1, n, stat_start, 0)
    lax.fori_loop(1, n, stat_wait, 0)
    parts = [stats[offset] for offset in range(n)]
    sums = sum(parts)
    norm_now = sums[:, 1:2]
    step_size = norm_now / sums[:, :1]
    wide_step = jnp.broadcast_to(step_size, shape)
    rests = 0.0
    for part in parts:
        gap = wide_step - jnp.broadcast_to(part[:, 4:5], shape)
        rests += part + gap * gap * jnp.broadcast_to(part[:, 3:4], shape)
    ratio = rests[:, 2:3] / norm_now
    residual = targets - step_size * image
    out_ref[:columns] = step_size * targets
    out_ref[columns : 2 * columns] = residual
    out_ref[2 * columns :] = residual + ratio * targets

    def finish(unit, _):
        phase = lax.rem(unit + 2, 4)
        ring = phase < 2

        @pl.when(ring)
        def _():
            chunk(0, 0, unit, 0, sibling).wait_send()
            chunk(0, 0, unit, 1, sibling).wait_send()

        @pl.when(jnp.logical_not(ring))
        def _():
            share(0, unit).wait_send()

        return 0

    lax.fori_loop(1, n, finish, 0)

    def stat_finish(offset, _):
        stat_copy(offset).wait_send()
        return 0

    lax.fori_loop(1, n, stat_finish, 0)


def spread(packed_ref, sol_ref, res_ref, dir_ref, sem):
    columns = sol_ref.shape[0]
    copies = [
        pltpu.make_async_copy(packed_ref.at[pl.ds(i * columns, columns)], ref, sem.at[i])
        for i, ref in enumerate((sol_ref, res_ref, dir_ref))
    ]
    for copy in copies:
        copy.start()
    for copy in copies:
        copy.wait()


def solution(mesh):
    n = mesh.shape["blk"]
    ladder = mesh.shape["groups"] == 2

    def body(points, targets, noise_var, inv_length):
        count, features = points.shape
        columns = targets.shape[1]
        out = jax.ShapeDtypeStruct((columns, count), F32)
        packed = pl.pallas_call(
            functools.partial(kernel, n, ladder),
            out_shape=jax.ShapeDtypeStruct((3 * columns, count), F32),
            in_specs=[pl.BlockSpec(memory_space=pl.ANY)] * 4,
            out_specs=pl.BlockSpec(memory_space=pltpu.VMEM),
            scratch_shapes=[
                pltpu.VMEM((n, 2, features + columns, count // 2), F32),
                pltpu.VMEM((features, count), F32),
                pltpu.VMEM((1, count), F32),
                pltpu.VMEM((1, features), F32),
                pltpu.VMEM((count, 6 * features + 16), BF16),
                pltpu.VMEM((count, 2 * columns), F32),
                pltpu.VMEM((n, columns, 128), F32),
                pltpu.SemaphoreType.DMA((2 * n,)),
                pltpu.SemaphoreType.DMA((2 * n,)),
                pltpu.SemaphoreType.DMA((5,)),
                pltpu.SemaphoreType.DMA((n,)),
                pltpu.SemaphoreType.DMA((n,)),
            ],
            compiler_params=pltpu.CompilerParams(collective_id=0, has_side_effects=True),
        )(points.T, targets.T, noise_var[None, :], inv_length[None, :])
        outs = pl.pallas_call(
            spread,
            out_shape=[out] * 3,
            in_specs=[pl.BlockSpec(memory_space=pltpu.VMEM)],
            out_specs=[pl.BlockSpec(memory_space=pl.ANY)] * 3,
            scratch_shapes=[pltpu.SemaphoreType.DMA((3,))],
        )(packed)
        return tuple(value.T for value in outs)

    rows, flat = P(("groups", "blk"), None), P(("groups", "blk"))
    return jax.shard_map(
        body,
        mesh=mesh,
        in_specs=(rows, rows, flat, P()),
        out_specs=(rows,) * 3,
        check_vma=False,
    )
```
